256 devices in a mesh: grp: 128 (over x_lo, z, y, core), half: 2 (over x_hi).
Axes of the slice: x: 4 (x_hi: 2, x_lo: 2; x = x_hi * 2 + x_lo), y: 4, z: 8, core: 2. Of those that a mesh axis runs over, the one named last changes fastest.
Arguments:
- field: bfloat16 [128, 2, 1024, 512], P('grp', 'half'), may hold values from -6 to 6
- source_one: bfloat16 [128, 2, 4, 256, 256], P('grp', 'half'), may hold values from -0.375 to 0.375
- sections_one: bfloat16 [128, 2, 3, 4, 256, 512], P('grp', 'half'), may hold values from -0.25 to 0.25
- target_one: bfloat16 [128, 2, 4, 256, 256], P('grp', 'half'), may hold values from -0.375 to 0.375
- source_two: bfloat16 [128, 2, 4, 256, 256], P('grp', 'half'), may hold values from -0.375 to 0.375
- sections_two: bfloat16 [128, 2, 3, 4, 256, 512], P('grp', 'half'), may hold values from -0.25 to 0.25
- target_two: bfloat16 [128, 2, 4, 256, 256], P('grp', 'half'), may hold values from -0.375 to 0.375
- pairing: int32 [2, 3, 128, 2, 4], P(None, None, 'grp', 'half'), may hold values from 0 to 3, each once within a row
Outputs:
- scattered: bfloat16 [128, 2, 1024, 512], P('grp', 'half')
The draws below stay inside these ranges and needn't reach their ends.
Inputs may be any that keep to these rules, and one draw needn't show every extreme that they name: For every level l, section s, group index g and half h, pairing[l, s, g, h] is a permutation of the 4 nodes.
All inputs are finite; a program needn't handle non-finite values.
Results may differ from the reference program's by a relative error of at most 0.007.
Values may be sent and summed in bfloat16 or wider, within the bound.
A program may use at most 64 MiB of HBM per device.

```python
import jax
import jax.numpy as jnp
import numpy as np

LEAF = 256
COLS = 512
NODES = 4
SECTIONS = 3
N_GRP = 128


def level_of(stream_key, dims, cuts, least, top_value):
    loudness = 1.0
    for axis_at, blocks in cuts:
        steps = jax.random.uniform(jax.random.fold_in(jax.random.fold_in(stream_key, 6), axis_at), (blocks,), jnp.float32, least / len(cuts), top_value / len(cuts))
        loudness = loudness * jnp.repeat(jnp.exp(steps), dims[axis_at] // blocks).reshape((-1,) + (1,) * (len(dims) - 1 - axis_at))
    return loudness


def normal_values(stream_key, dims, width, bound, pieces=(), kind=jnp.bfloat16):
    loudness = level_of(stream_key, dims, pieces, -0.22, 0.18) if pieces else 1.0
    array = jax.random.normal(stream_key, dims, jnp.float32) * width * loudness
    return jnp.minimum(jnp.maximum(array, -bound), bound).astype(kind)


def setup_inputs(seed: int = 0) -> dict:
    seeds = jax.random.split(jax.random.key(seed), 9)
    return {
        "field": normal_values(seeds[0], (N_GRP, 2, NODES * LEAF, COLS), 1.0, 6.0, ((0, 128), (1, 2))),
        "source_one": normal_values(seeds[1], (N_GRP, 2, NODES, LEAF, LEAF), LEAF ** -0.5, 0.375, ((0, 128), (1, 2))),
        "sections_one": normal_values(seeds[2], (N_GRP, 2, SECTIONS, NODES, LEAF, 2 * LEAF), (2 * LEAF) ** -0.5, 0.25, ((0, 128), (1, 2))),
        "target_one": normal_values(seeds[3], (N_GRP, 2, NODES, LEAF, LEAF), LEAF ** -0.5, 0.375, ((0, 128), (1, 2))),
        "source_two": normal_values(seeds[4], (N_GRP, 2, NODES, LEAF, LEAF), LEAF ** -0.5, 0.375, ((0, 128), (1, 2))),
        "sections_two": normal_values(seeds[5], (N_GRP, 2, SECTIONS, NODES, LEAF, 2 * LEAF), (2 * LEAF) ** -0.5, 0.25, ((0, 128), (1, 2))),
        "target_two": normal_values(seeds[6], (N_GRP, 2, NODES, LEAF, LEAF), LEAF ** -0.5, 0.375, ((0, 128), (1, 2))),
        "pairing": jax.vmap(lambda own: jax.random.permutation(own, NODES))(jax.random.split(seeds[7], 2 * SECTIONS * N_GRP * 2)).reshape((2, SECTIONS, N_GRP, 2, NODES)).astype(jnp.int32),
    }


def leaf_product(basis, blocks):
    return jnp.einsum('ghnij,ghnjc->ghnic', basis.astype(jnp.float32), blocks.astype(jnp.float32))


def run_sections(coeffs, weights, tables, first_bit):
    for section in range(SECTIONS):
        partner_rows = np.arange(N_GRP) ^ (1 << (first_bit - section))
        partner = coeffs[partner_rows]
        index = jnp.broadcast_to(tables[section].astype(jnp.int32)[:, :, :, None, None], partner.shape)
        partner = jnp.take_along_axis(partner, index, axis=2)
        stacked = jnp.concatenate([coeffs, partner], axis=3)
        coeffs = leaf_product(weights[:, :, section], stacked).astype(jnp.bfloat16)
    return coeffs


def reference(field, source_one, sections_one, target_one, source_two, sections_two, target_two, pairing):
    top_bit = N_GRP.bit_length() - 1
    shaped = field.reshape(N_GRP, 2, NODES, LEAF, COLS)
    first = run_sections(leaf_product(source_one, shaped).astype(jnp.bfloat16), sections_one, pairing[0], top_bit - 1)
    second = run_sections(leaf_product(source_two, shaped).astype(jnp.bfloat16), sections_two, pairing[1], top_bit - 2)
    far_rows = np.arange(N_GRP) ^ (N_GRP // 2)
    total = leaf_product(target_one, first[:, ::-1]) + leaf_product(target_two, second[far_rows])
    return total.astype(jnp.bfloat16).reshape(N_GRP, 2, NODES * LEAF, COLS)
```

```python
import functools

import jax
import jax.numpy as jnp
from jax import lax
from jax.experimental import pallas as pl
from jax.experimental.pallas import tpu as pltpu
from jax.sharding import PartitionSpec as P

SECTIONS = 3
STAGES = SECTIONS + 1
WIDTH = 128
MESH = pl.DeviceIdType.MESH
WINDOW = 2
ONE, TWO = 0, 1
CRITICAL = ((TWO, 0), (ONE, 1), (TWO, 1), (ONE, 2))


def flipped(index, bit):
    size = 1 << bit
    return index + size - 2 * size * ((index // size) % 2)


def arrivals(chunks):
    due = []
    span = 2.0
    for place, (level, stage) in enumerate(CRITICAL):
        for c in range(chunks):
            due.append((span * (chunks * place + c + 1), level, stage, c))
    for c in range(chunks):
        due.append((c + 1.0 + 0.1, ONE, 0, c))
        done = span * (2 * chunks + c + 1)
        due.append((done + 1.5 * span, TWO, 2, c))
        done = span * (3 * chunks + c + 1)
        due.append((done + 1.5 * span, ONE, 3, c))
    return [entry[1:] for entry in sorted(due)]


def kernel(
    top_bit, field, source_one, sections_one, target_one, source_two, sections_two, target_two, tables,
    out, x, sources, weights, targets, own, last, total,
    in_sems, out_sems, send_sems, recv_sems, node_send_sems, node_recv_sems, *landings,
):
    nodes, chunks = own.shape[3], own.shape[2]
    leaf = x.shape[1]
    g, h = lax.axis_index("grp"), lax.axis_index("half")

    landing = iter(landings)
    partner = {
        (level, s, c): next(landing)
        for level in (ONE, TWO) for s in range(SECTIONS) for c in range(chunks)
    }
    for level in (ONE, TWO):
        for c in range(chunks):
            partner[level, SECTIONS, c] = last.at[level, c]

    loads = {}

    def load(name, at, src, dst):
        loads[name] = pltpu.make_async_copy(src, dst, in_sems.at[at])
        loads[name].start()

    load("x", 0, field, x)
    load(("s", TWO), 1, source_two, sources.at[TWO])
    load(("s", ONE), 2, source_one, sources.at[ONE])
    for s in range(SECTIONS):
        load(("w", ONE, s), 3 + 2 * s, sections_one.at[s], weights.at[ONE, s])
        load(("w", TWO, s), 4 + 2 * s, sections_two.at[s], weights.at[TWO, s])
    load(("t", ONE), 9, target_one, targets.at[ONE])
    load(("t", TWO), 10, target_two, targets.at[TWO])

    def need(name):
        if name in loads:
            loads.pop(name).wait()

    peers = {}
    for s in range(SECTIONS):
        peers[ONE, s] = (flipped(g, top_bit - 1 - s), h)
        peers[TWO, s] = (flipped(g, top_bit - 2 - s), h)
    peers[ONE, SECTIONS] = (g, 1 - h)
    peers[TWO, SECTIONS] = (flipped(g, top_bit - 1), h)

    barrier = pltpu.get_barrier_semaphore()
    greeted = [peers[ONE, s] for s in range(STAGES)] + [peers[TWO, 2]]
    for peer in greeted:
        pl.semaphore_signal(barrier, inc=1, device_id=peer, device_id_type=MESH)

    def move(level, stage, c):
        return pltpu.make_async_remote_copy(
            src_ref=own.at[level, stage, c],
            dst_ref=partner[level, stage, c],
            send_sem=send_sems.at[level, stage, c],
            recv_sem=recv_sems.at[level, stage, c],
            device_id=peers[level, stage],
            device_id_type=MESH,
        )

    def move_node(c, n):
        return pltpu.make_async_remote_copy(
            src_ref=own.at[ONE, SECTIONS, c, n],
            dst_ref=last.at[ONE, c, n],
            send_sem=node_send_sems.at[c, n],
            recv_sem=node_recv_sems.at[c, n],
            device_id=peers[ONE, SECTIONS],
            device_id_type=MESH,
        )

    def start_leaves(level, c):
        need("x")
        need(("s", level))

        @pl.loop(0, nodes)
        def _(n):
            block = x[n, :, c * WIDTH : (c + 1) * WIDTH]
            own[level, 0, c, n] = jnp.dot(
                sources[level, n], block, preferred_element_type=jnp.float32
            ).astype(jnp.bfloat16)

    def section(level, s, c):
        need(("w", level, s))

        @pl.loop(0, nodes)
        def _(n):
            near = jnp.dot(
                weights[level, s, n, :, :leaf], own[level, s, c, n], preferred_element_type=jnp.float32
            )
            far = jnp.dot(
                weights[level, s, n, :, leaf:],
                partner[level, s, c][tables[level, s, 0, 0, n]],
                preferred_element_type=jnp.float32,
            )
            own[level, s + 1, c, n] = (near + far).astype(jnp.bfloat16)
            if (level, s) == (ONE, SECTIONS - 1):
                move_node(c, n).start()

    def finish(c):
        need(("t", ONE))
        need(("t", TWO))
        move(TWO, SECTIONS, c).wait_recv()

        @pl.loop(0, nodes)
        def _(n):
            move_node(c, n).wait_recv()
            one = jnp.dot(
                targets[ONE, n], last[ONE, c, n], preferred_element_type=jnp.float32
            )
            two = jnp.dot(
                targets[TWO, n], last[TWO, c, n], preferred_element_type=jnp.float32
            )
            total[n, :, c * WIDTH : (c + 1) * WIDTH] = (one + two).astype(jnp.bfloat16)

        store(c).start()

    def store(c):
        columns = pl.ds(c * WIDTH, WIDTH)
        return pltpu.make_async_copy(total.at[:, :, columns], out.at[:, :, columns], out_sems.at[c])

    order = [(level, stage, c) for level, stage in CRITICAL for c in range(chunks)]
    ready, sent, received = set(), 0, 0
    greeting = [True]

    def greet():
        if greeting:
            greeting.pop()
            pl.semaphore_wait(barrier, len(greeted))

    def push():
        nonlocal sent
        while sent < len(order) and order[sent] in ready and sent < received + WINDOW:
            greet()
            move(*order[sent]).start()
            sent += 1

    for c in range(chunks):
        start_leaves(TWO, c)
        ready.add((TWO, 0, c))
        push()
        start_leaves(ONE, c)
        move(ONE, 0, c).start()
    for level, stage, c in arrivals(chunks):
        if (level, stage) == (ONE, SECTIONS):
            finish(c)
            continue
        move(level, stage, c).wait_recv()
        if (level, stage, c) in order:
            received += 1
            push()
        section(level, stage, c)
        ready.add((level, stage + 1, c))
        push()
        if (level, stage + 1) not in CRITICAL and (level, stage + 1) != (ONE, SECTIONS):
            move(level, stage + 1, c).start()

    for c in range(chunks):
        for level in (ONE, TWO):
            for stage in range(STAGES):
                if (level, stage) != (ONE, SECTIONS):
                    move(level, stage, c).wait_send()
        for n in range(nodes):
            move_node(c, n).wait_send()
        store(c).wait()


def on_device(
    field, source_one, sections_one, target_one, source_two, sections_two, target_two, pairing
):
    nodes, leaf = source_one.shape[2:4]
    columns = field.shape[3]
    chunks = columns // WIDTH
    top_bit = lax.axis_size("grp").bit_length() - 1
    anywhere = pl.BlockSpec(memory_space=pl.ANY)
    half = jnp.bfloat16
    blocks = (2, STAGES, chunks, nodes, leaf, WIDTH)
    result = pl.pallas_call(
        functools.partial(kernel, top_bit),
        out_shape=jax.ShapeDtypeStruct((nodes, leaf, columns), half),
        in_specs=[anywhere] * 7 + [pl.BlockSpec(memory_space=pltpu.SMEM)],
        out_specs=anywhere,
        scratch_shapes=[
            pltpu.VMEM((nodes, leaf, columns), half),
            pltpu.VMEM((2, nodes, leaf, leaf), half),
            pltpu.VMEM((2, SECTIONS, nodes, leaf, 2 * leaf), half),
            pltpu.VMEM((2, nodes, leaf, leaf), half),
            pltpu.VMEM(blocks, half),
            pltpu.VMEM((2, chunks, nodes, leaf, WIDTH), half),
            pltpu.VMEM((nodes, leaf, columns), half),
            pltpu.SemaphoreType.DMA((11,)),
            pltpu.SemaphoreType.DMA((chunks,)),
            pltpu.SemaphoreType.DMA((2, STAGES, chunks)),
            pltpu.SemaphoreType.DMA((2, STAGES, chunks)),
            pltpu.SemaphoreType.DMA((chunks, nodes)),
            pltpu.SemaphoreType.DMA((chunks, nodes)),
        ]
        + [pltpu.VMEM((nodes, leaf, WIDTH), half)] * (2 * SECTIONS * chunks),
        compiler_params=pltpu.CompilerParams(
            collective_id=0, has_side_effects=True, vmem_limit_bytes=56 << 20
        ),
        name="butterfly",
    )(
        field.reshape(nodes, leaf, columns),
        source_one[0, 0], sections_one[0, 0], target_one[0, 0],
        source_two[0, 0], sections_two[0, 0], target_two[0, 0],
        pairing,
    )
    return result.reshape(field.shape)


def solution(mesh):
    placed = (
        P("grp", "half", None, None),
        P("grp", "half", None, None, None),
        P("grp", "half", None, None, None, None),
        P("grp", "half", None, None, None),
        P("grp", "half", None, None, None),
        P("grp", "half", None, None, None, None),
        P("grp", "half", None, None, None),
        P(None, None, "grp", "half", None),
    )
    return jax.shard_map(
        on_device,
        mesh=mesh,
        in_specs=placed,
        out_specs=P("grp", "half", None, None),
        check_vma=False,
    )
```

```python
import functools

import jax
import jax.numpy as jnp
from jax import lax
from jax.experimental import pallas as pl
from jax.experimental.pallas import tpu as pltpu
from jax.sharding import PartitionSpec as P

SECTIONS = 3
STAGES = SECTIONS + 1
WIDTH = 128
MESH = pl.DeviceIdType.MESH
WINDOW = 2
ONE, TWO = 0, 1
CRITICAL = ((TWO, 0), (ONE, 1), (TWO, 1), (ONE, 2))
LENT = 3


def flipped(index, bit):
    size = 1 << bit
    return index + size - 2 * size * ((index // size) % 2)


def arrivals(chunks):
    due = []
    span = 2.0
    for place, (level, stage) in enumerate(CRITICAL):
        for c in range(chunks):
            due.append((span * (chunks * place + c + 1), level, stage, c))
    for c in range(chunks):
        due.append((c + 1.0 + 0.1, ONE, 0, c))
        done = span * (2 * chunks + c + 1)
        due.append((done + 1.5 * span, TWO, 2, c))
        due.append((span * (chunks + c + 1) + 1.5 * span, ONE, LENT, c))
    return [entry[1:] for entry in sorted(due)]


def kernel(
    top_bit, field, source_one, sections_one, target_one, source_two, sections_two, target_two, tables,
    out, x, sources, weights, lent, targets, own, last, total, table, lent_table,
    in_sems, out_sems, send_sems, recv_sems, lent_send_sems, lent_recv_sems, *landings,
):
    nodes, chunks = own.shape[3], own.shape[2]
    leaf = x.shape[1]
    g, h = lax.axis_index("grp"), lax.axis_index("half")

    landing = iter(landings)
    partner = {
        (level, s, c): next(landing)
        for level in (ONE, TWO) for s in range(SECTIONS) for c in range(chunks)
    }
    for c in range(chunks):
        partner[ONE, LENT, c] = last.at[ONE, c]
        partner[TWO, SECTIONS, c] = last.at[TWO, c]

    loads = {}

    def load(name, src, dst):
        loads[name] = pltpu.make_async_copy(src, dst, in_sems.at[len(all_loads)])
        all_loads.append(name)
        loads[name].start()

    all_loads = []
    for c in range(chunks):
        columns = pl.ds(c * WIDTH, WIDTH)
        load(("x", c), field.at[:, :, columns], x.at[:, :, columns])
        if c == 0:
            load(("s", TWO), source_two, sources.at[TWO])
            load(("s", ONE), source_one, sources.at[ONE])

    def load_rest():
        load("tables", tables, table)
        for s in range(SECTIONS):
            if s < SECTIONS - 1:
                load(("w", ONE, s), sections_one.at[s], weights.at[ONE, s])
            load(("w", TWO, s), sections_two.at[s], weights.at[TWO, s])
        load(("t", ONE), target_one, targets.at[ONE])
        load(("t", TWO), target_two, targets.at[TWO])

    def need(name):
        if name in loads:
            loads.pop(name).wait()

    peers = {}
    for s in range(SECTIONS):
        peers[ONE, s] = (flipped(g, top_bit - 1 - s), h)
        peers[TWO, s] = (flipped(g, top_bit - 2 - s), h)
    peers[ONE, LENT] = (g, 1 - h)
    peers[ONE, SECTIONS - 1] = (peers[ONE, SECTIONS - 1][0], 1 - h)
    peers[TWO, SECTIONS] = (flipped(g, top_bit - 1), h)

    barrier = pltpu.get_barrier_semaphore()
    greeted = [peers[ONE, s] for s in range(STAGES)] + [peers[TWO, 1], peers[TWO, 2]]
    for peer in greeted:
        pl.semaphore_signal(barrier, inc=1, device_id=peer, device_id_type=MESH)

    def move(level, stage, c):
        return pltpu.make_async_remote_copy(
            src_ref=own.at[level, 2 if (level, stage) == (ONE, LENT) else stage, c],
            dst_ref=partner[level, stage, c],
            send_sem=send_sems.at[level, stage, c],
            recv_sem=recv_sems.at[level, stage, c],
            device_id=peers[level, stage],
            device_id_type=MESH,
        )

    def lend(at, src, dst):
        return pltpu.make_async_remote_copy(
            src_ref=src,
            dst_ref=dst,
            send_sem=lent_send_sems.at[at],
            recv_sem=lent_recv_sems.at[at],
            device_id=peers[ONE, LENT],
            device_id_type=MESH,
        )

    lending = [lend(0, sections_one.at[SECTIONS - 1], lent), lend(1, tables, lent_table)]

    def start_leaves(level, c):
        need(("x", c))
        need(("s", level))

        @pl.loop(0, nodes)
        def _(n):
            block = x[n, :, c * WIDTH : (c + 1) * WIDTH]
            own[level, 0, c, n] = jnp.dot(
                sources[level, n], block, preferred_element_type=jnp.float32
            ).astype(jnp.bfloat16)

    def section(level, s, c):
        need(("w", level, s))
        need("tables")

        @pl.loop(0, nodes)
        def _(n):
            near = jnp.dot(
                weights[level, s, n, :, :leaf], own[level, s, c, n], preferred_element_type=jnp.float32
            )
            far = jnp.dot(
                weights[level, s, n, :, leaf:],
                partner[level, s, c][table[level, s, 0, 0, n]],
                preferred_element_type=jnp.float32,
            )
            own[level, s + 1, c, n] = (near + far).astype(jnp.bfloat16)

    def finish(c):
        need(("t", ONE))
        need(("t", TWO))

        @pl.loop(0, nodes)
        def _(n):
            near = jnp.dot(lent[n, :, :leaf], last[ONE, c, n], preferred_element_type=jnp.float32)
            far = jnp.dot(
                lent[n, :, leaf:],
                partner[ONE, 2, c][lent_table[ONE, 2, 0, 0, n]],
                preferred_element_type=jnp.float32,
            )
            one = jnp.dot(
                targets[ONE, n], (near + far).astype(jnp.bfloat16), preferred_element_type=jnp.float32
            )
            two = jnp.dot(targets[TWO, n], last[TWO, c, n], preferred_element_type=jnp.float32)
            total[n, :, c * WIDTH : (c + 1) * WIDTH] = (one + two).astype(jnp.bfloat16)

        store(c).start()

    def store(c):
        columns = pl.ds(c * WIDTH, WIDTH)
        return pltpu.make_async_copy(total.at[:, :, columns], out.at[:, :, columns], out_sems.at[c])

    order = [(level, stage, c) for level, stage in CRITICAL for c in range(chunks)]
    ready, sent, received = set(), 0, 0
    greeting = [True]

    def greet():
        if greeting:
            greeting.pop()
            pl.semaphore_wait(barrier, len(greeted))

    def push():
        nonlocal sent
        while sent < len(order) and order[sent] in ready and sent < received + WINDOW:
            greet()
            move(*order[sent]).start()
            sent += 1

    for c in range(chunks):
        start_leaves(TWO, c)
        ready.add((TWO, 0, c))
        push()
        start_leaves(ONE, c)
        move(ONE, 0, c).start()
        if c == 0:
            load_rest()
    for level, stage, c in arrivals(chunks):
        if (level, stage) == (ONE, 2):
            move(TWO, SECTIONS, c).wait_recv()
            if c == 0:
                for copy in lending:
                    copy.wait_recv()
        move(level, stage, c).wait_recv()
        if (level, stage, c) in order:
            received += 1
            push()
        if (level, stage) == (ONE, LENT):
            continue
        if (level, stage) == (ONE, 2):
            finish(c)
            continue
        section(level, stage, c)
        if (level, stage, c) == (ONE, 0, chunks - 1):
            for copy in lending:
                copy.start()
        ready.add((level, stage + 1, c))
        push()
        if (level, stage) == (ONE, 1):
            move(ONE, LENT, c).start()
        if (level, stage + 1) not in CRITICAL:
            move(level, stage + 1, c).start()

    for copy in lending:
        copy.wait_send()
    for c in range(chunks):
        for level in (ONE, TWO):
            for stage in range(STAGES):
                move(level, stage, c).wait_send()
        store(c).wait()


def on_device(
    field, source_one, sections_one, target_one, source_two, sections_two, target_two, pairing
):
    nodes, leaf = source_one.shape[2:4]
    columns = field.shape[3]
    chunks = columns // WIDTH
    top_bit = lax.axis_size("grp").bit_length() - 1
    anywhere = pl.BlockSpec(memory_space=pl.ANY)
    half = jnp.bfloat16
    blocks = (2, STAGES, chunks, nodes, leaf, WIDTH)
    result = pl.pallas_call(
        functools.partial(kernel, top_bit),
        out_shape=jax.ShapeDtypeStruct((nodes, leaf, columns), half),
        in_specs=[anywhere] * 8,
        out_specs=anywhere,
        scratch_shapes=[
            pltpu.VMEM((nodes, leaf, columns), half),
            pltpu.VMEM((2, nodes, leaf, leaf), half),
            pltpu.VMEM((2, SECTIONS, nodes, leaf, 2 * leaf), half),
            pltpu.VMEM((nodes, leaf, 2 * leaf), half),
            pltpu.VMEM((2, nodes, leaf, leaf), half),
            pltpu.VMEM(blocks, half),
            pltpu.VMEM((2, chunks, nodes, leaf, WIDTH), half),
            pltpu.VMEM((nodes, leaf, columns), half),
            pltpu.SMEM(pairing.shape, pairing.dtype),
            pltpu.SMEM(pairing.shape, pairing.dtype),
            pltpu.SemaphoreType.DMA((chunks + 2 + 1 + 2 * SECTIONS - 1 + 2,)),
            pltpu.SemaphoreType.DMA((chunks,)),
            pltpu.SemaphoreType.DMA((2, STAGES, chunks)),
            pltpu.SemaphoreType.DMA((2, STAGES, chunks)),
            pltpu.SemaphoreType.DMA((2,)),
            pltpu.SemaphoreType.DMA((2,)),
        ]
        + [pltpu.VMEM((nodes, leaf, WIDTH), half)] * (2 * SECTIONS * chunks),
        compiler_params=pltpu.CompilerParams(
            collective_id=0, has_side_effects=True, vmem_limit_bytes=56 << 20
        ),
        name="butterfly",
    )(
        field.reshape(nodes, leaf, columns),
        source_one[0, 0], sections_one[0, 0], target_one[0, 0],
        source_two[0, 0], sections_two[0, 0], target_two[0, 0],
        pairing,
    )
    return result.reshape(field.shape)


def solution(mesh):
    placed = (
        P("grp", "half", None, None),
        P("grp", "half", None, None, None),
        P("grp", "half", None, None, None, None),
        P("grp", "half", None, None, None),
        P("grp", "half", None, None, None),
        P("grp", "half", None, None, None, None),
        P("grp", "half", None, None, None),
        P(None, None, "grp", "half", None),
    )
    return jax.shard_map(
        on_device,
        mesh=mesh,
        in_specs=placed,
        out_specs=P("grp", "half", None, None),
        check_vma=False,
    )
```

```python
import functools

import jax
import jax.numpy as jnp
from jax import lax
from jax.experimental import pallas as pl
from jax.experimental.pallas import tpu as pltpu
from jax.sharding import PartitionSpec as P

SECTIONS = 3
STAGES = SECTIONS + 1
WIDTH = 128
MESH = pl.DeviceIdType.MESH
WINDOW = 2
ONE, TWO = 0, 1
CRITICAL = ((TWO, 0), (ONE, 1), (TWO, 1), (ONE, 2))
LENT = 3


def flipped(index, bit):
    size = 1 << bit
    return index + size - 2 * size * ((index // size) % 2)


def arrivals(chunks):
    due = []
    span = 2.0
    for place, (level, stage) in enumerate(CRITICAL):
        for c in range(chunks):
            due.append((span * (chunks * place + c + 1), level, stage, c))
    for c in range(chunks):
        due.append((c + 1.0 + 0.1, ONE, 0, c))
        done = span * (2 * chunks + c + 1)
        due.append((done + 1.5 * span, TWO, 2, c))
        due.append((span * (chunks + c + 1) + 1.5 * span, ONE, LENT, c))
    return [entry[1:] for entry in sorted(due)]


def kernel(
    top_bit, field, source_one, sections_one, target_one, source_two, sections_two, target_two, tables,
    out, x, sources, weights, lent, targets, own, last, near, one, two, total, table, lent_table,
    in_sems, out_sems, send_sems, recv_sems, lent_send_sems, lent_recv_sems, *landings,
):
    nodes, chunks = own.shape[3], own.shape[2]
    leaf = x.shape[1]
    g, h = lax.axis_index("grp"), lax.axis_index("half")

    peers = {}
    for s in range(SECTIONS):
        peers[ONE, s] = (flipped(g, top_bit - 1 - s), h)
        peers[TWO, s] = (flipped(g, top_bit - 2 - s), h)
    peers[ONE, LENT] = (g, 1 - h)
    peers[ONE, SECTIONS - 1] = (peers[ONE, SECTIONS - 1][0], 1 - h)
    peers[TWO, SECTIONS] = (flipped(g, top_bit - 1), h)

    barrier = pltpu.get_barrier_semaphore()
    greeted = [peers[ONE, s] for s in range(STAGES)] + [peers[TWO, 1], peers[TWO, 2]]
    for peer in greeted:
        pl.semaphore_signal(barrier, inc=1, device_id=peer, device_id_type=MESH)

    landing = iter(landings)
    partner = {
        (level, s, c): next(landing)
        for level in (ONE, TWO) for s in range(SECTIONS) for c in range(chunks)
    }
    for c in range(chunks):
        partner[ONE, LENT, c] = last.at[ONE, c]
        partner[TWO, SECTIONS, c] = last.at[TWO, c]

    loads = {}

    def load(name, src, dst):
        loads[name] = pltpu.make_async_copy(src, dst, in_sems.at[len(all_loads)])
        all_loads.append(name)
        loads[name].start()

    all_loads = []
    for c in range(chunks):
        columns = pl.ds(c * WIDTH, WIDTH)
        load(("x", c), field.at[:, :, columns], x.at[:, :, columns])
        if c == 0:
            load(("s", TWO), source_two, sources.at[TWO])
            load(("s", ONE), source_one, sources.at[ONE])

    def load_rest():
        load("tables", tables, table)
        for s in range(SECTIONS):
            if s < SECTIONS - 1:
                load(("w", ONE, s), sections_one.at[s], weights.at[ONE, s])
            load(("w", TWO, s), sections_two.at[s], weights.at[TWO, s])
        load(("t", ONE), target_one, targets.at[ONE])
        load(("t", TWO), target_two, targets.at[TWO])

    def need(name):
        if name in loads:
            loads.pop(name).wait()

    def move(level, stage, c):
        return pltpu.make_async_remote_copy(
            src_ref=own.at[level, 2 if (level, stage) == (ONE, LENT) else stage, c],
            dst_ref=partner[level, stage, c],
            send_sem=send_sems.at[level, stage, c],
            recv_sem=recv_sems.at[level, stage, c],
            device_id=peers[level, stage],
            device_id_type=MESH,
        )

    def lend(at, src, dst):
        return pltpu.make_async_remote_copy(
            src_ref=src,
            dst_ref=dst,
            send_sem=lent_send_sems.at[at],
            recv_sem=lent_recv_sems.at[at],
            device_id=peers[ONE, LENT],
            device_id_type=MESH,
        )

    lending = [lend(0, sections_one.at[SECTIONS - 1], lent), lend(1, tables, lent_table)]

    def start_leaves(level, c):
        need(("x", c))
        need(("s", level))

        @pl.loop(0, nodes)
        def _(n):
            block = x[n, :, c * WIDTH : (c + 1) * WIDTH]
            own[level, 0, c, n] = jnp.dot(
                sources[level, n], block, preferred_element_type=jnp.float32
            ).astype(jnp.bfloat16)

    def section(level, s, c):
        need(("w", level, s))
        need("tables")

        @pl.loop(0, nodes)
        def _(n):
            near = jnp.dot(
                weights[level, s, n, :, :leaf], own[level, s, c, n], preferred_element_type=jnp.float32
            )
            far = jnp.dot(
                weights[level, s, n, :, leaf:],
                partner[level, s, c][table[level, s, 0, 0, n]],
                preferred_element_type=jnp.float32,
            )
            own[level, s + 1, c, n] = (near + far).astype(jnp.bfloat16)

    def prepare(c):
        need(("t", TWO))

        @pl.loop(0, nodes)
        def _(n):
            near[n] = jnp.dot(lent[n, :, :leaf], last[ONE, c, n], preferred_element_type=jnp.float32)
            two[n] = jnp.dot(targets[TWO, n], last[TWO, c, n], preferred_element_type=jnp.float32)

    def finish(c):
        need(("t", ONE))
        for n in range(nodes):
            far = jnp.dot(
                lent[n, :, leaf:],
                partner[ONE, 2, c][lent_table[ONE, 2, 0, 0, n]],
                preferred_element_type=jnp.float32,
            )
            one[n] = (near[n] + far).astype(jnp.bfloat16)
        for n in range(nodes):
            product = jnp.dot(targets[ONE, n], one[n], preferred_element_type=jnp.float32)
            total[n, :, c * WIDTH : (c + 1) * WIDTH] = (product + two[n]).astype(jnp.bfloat16)
            store(c, n).start()

    def store(c, n):
        columns = pl.ds(c * WIDTH, WIDTH)
        return pltpu.make_async_copy(total.at[n, :, columns], out.at[n, :, columns], out_sems.at[c, n])

    order = [(level, stage, c) for level, stage in CRITICAL for c in range(chunks)]
    moves = [
        (level, stage) for level in (ONE, TWO) for stage in range(STAGES) if (level, stage) != (ONE, 2)
    ]
    ready, sent, received = set(), 0, 0
    greeting = [True]

    def greet():
        if greeting:
            greeting.pop()
            pl.semaphore_wait(barrier, len(greeted))

    def push():
        nonlocal sent
        while sent < len(order) and order[sent] in ready and sent < received + WINDOW:
            greet()
            move(*order[sent]).start()
            sent += 1

    for c in range(chunks):
        start_leaves(TWO, c)
        ready.add((TWO, 0, c))
        push()
        start_leaves(ONE, c)
        move(ONE, 0, c).start()
        if c == 0:
            load_rest()
    for level, stage, c in arrivals(chunks):
        if (level, stage) == (ONE, 2):
            move(TWO, SECTIONS, c).wait_recv()
            if c == 0:
                for copy in lending:
                    copy.wait_recv()
            prepare(c)
            if c == chunks - 1:
                for copy in lending:
                    copy.wait_send()
                for at in range(chunks):
                    for there in moves:
                        move(*there, at).wait_send()
        move(level, stage, c).wait_recv()
        if (level, stage, c) in order:
            received += 1
            push()
        if (level, stage) == (ONE, LENT):
            continue
        if (level, stage) == (ONE, 2):
            finish(c)
            continue
        section(level, stage, c)
        if (level, stage, c) == (ONE, 0, chunks - 1):
            for copy in lending:
                copy.start()
        ready.add((level, stage + 1, c))
        push()
        if (level, stage) == (ONE, 1):
            move(ONE, LENT, c).start()
        if (level, stage + 1) not in CRITICAL:
            move(level, stage + 1, c).start()

    for c in range(chunks):
        move(ONE, 2, c).wait_send()
        for n in range(nodes):
            store(c, n).wait()


def on_device(
    field, source_one, sections_one, target_one, source_two, sections_two, target_two, pairing
):
    nodes, leaf = source_one.shape[2:4]
    columns = field.shape[3]
    chunks = columns // WIDTH
    top_bit = lax.axis_size("grp").bit_length() - 1
    anywhere = pl.BlockSpec(memory_space=pl.ANY)
    half = jnp.bfloat16
    blocks = (2, STAGES, chunks, nodes, leaf, WIDTH)
    result = pl.pallas_call(
        functools.partial(kernel, top_bit),
        out_shape=jax.ShapeDtypeStruct((nodes, leaf, columns), half),
        in_specs=[anywhere] * 8,
        out_specs=anywhere,
        scratch_shapes=[
            pltpu.VMEM((nodes, leaf, columns), half),
            pltpu.VMEM((2, nodes, leaf, leaf), half),
            pltpu.VMEM((2, SECTIONS, nodes, leaf, 2 * leaf), half),
            pltpu.VMEM((nodes, leaf, 2 * leaf), half),
            pltpu.VMEM((2, nodes, leaf, leaf), half),
            pltpu.VMEM(blocks, half),
            pltpu.VMEM((2, chunks, nodes, leaf, WIDTH), half),
            pltpu.VMEM((nodes, leaf, WIDTH), jnp.float32),
            pltpu.VMEM((nodes, leaf, WIDTH), half),
            pltpu.VMEM((nodes, leaf, WIDTH), jnp.float32),
            pltpu.VMEM((nodes, leaf, columns), half),
            pltpu.SMEM(pairing.shape, pairing.dtype),
            pltpu.SMEM(pairing.shape, pairing.dtype),
            pltpu.SemaphoreType.DMA((chunks + 2 + 1 + 2 * SECTIONS - 1 + 2,)),
            pltpu.SemaphoreType.DMA((chunks, nodes)),
            pltpu.SemaphoreType.DMA((2, STAGES, chunks)),
            pltpu.SemaphoreType.DMA((2, STAGES, chunks)),
            pltpu.SemaphoreType.DMA((2,)),
            pltpu.SemaphoreType.DMA((2,)),
        ]
        + [pltpu.VMEM((nodes, leaf, WIDTH), half)] * (2 * SECTIONS * chunks),
        compiler_params=pltpu.CompilerParams(
            collective_id=0, has_side_effects=True, vmem_limit_bytes=56 << 20
        ),
        name="butterfly",
    )(
        field.reshape(nodes, leaf, columns),
        source_one[0, 0], sections_one[0, 0], target_one[0, 0],
        source_two[0, 0], sections_two[0, 0], target_two[0, 0],
        pairing,
    )
    return result.reshape(field.shape)


def solution(mesh):
    placed = (
        P("grp", "half", None, None),
        P("grp", "half", None, None, None),
        P("grp", "half", None, None, None, None),
        P("grp", "half", None, None, None),
        P("grp", "half", None, None, None),
        P("grp", "half", None, None, None, None),
        P("grp", "half", None, None, None),
        P(None, None, "grp", "half", None),
    )
    return jax.shard_map(
        on_device,
        mesh=mesh,
        in_specs=placed,
        out_specs=P("grp", "half", None, None),
        check_vma=False,
    )
```

```python
import functools

import jax
import jax.numpy as jnp
from jax import lax
from jax.experimental import pallas as pl
from jax.experimental.pallas import tpu as pltpu
from jax.sharding import PartitionSpec as P

SECTIONS = 3
STAGES = SECTIONS + 1
WIDTH = 128
MESH = pl.DeviceIdType.MESH
WINDOW = 2
ONE, TWO = 0, 1
CRITICAL = ((TWO, 0), (ONE, 1), (TWO, 1), (ONE, 2))
LENT = 3


def flipped(index, bit):
    size = 1 << bit
    return index + size - 2 * size * ((index // size) % 2)


def arrivals(chunks):
    due = []
    span = 2.0
    for place, (level, stage) in enumerate(CRITICAL):
        for c in range(chunks):
            due.append((span * (chunks * place + c + 1), level, stage, c))
    for c in range(chunks):
        due.append((c + 1.0 + 0.1, ONE, 0, c))
        done = span * (2 * chunks + c + 1)
        due.append((done + 1.5 * span, TWO, 2, c))
        due.append((span * (chunks + c + 1) + 1.5 * span, ONE, LENT, c))
    return [entry[1:] for entry in sorted(due)]


def kernel(
    top_bit, field, source_one, sections_one, target_one, source_two, sections_two, target_two, tables,
    *results_and_scratch,
):
    nodes = source_one.shape[0]
    outs = results_and_scratch[:nodes]
    (
        x, sources, weights, lent, targets, own, last, near, one, two, table, lent_table,
        in_sems, send_sems, recv_sems, lent_send_sems, lent_recv_sems, *landings,
    ) = results_and_scratch[nodes:]
    chunks = own.shape[2]
    leaf = x.shape[1]
    g, h = lax.axis_index("grp"), lax.axis_index("half")

    peers = {}
    for s in range(SECTIONS):
        peers[ONE, s] = (flipped(g, top_bit - 1 - s), h)
        peers[TWO, s] = (flipped(g, top_bit - 2 - s), h)
    peers[ONE, LENT] = (g, 1 - h)
    peers[ONE, SECTIONS - 1] = (peers[ONE, SECTIONS - 1][0], 1 - h)
    peers[TWO, SECTIONS] = (flipped(g, top_bit - 1), h)

    barrier = pltpu.get_barrier_semaphore()
    greeted = [peers[ONE, s] for s in range(STAGES)] + [peers[TWO, 1], peers[TWO, 2]]
    for peer in greeted:
        pl.semaphore_signal(barrier, inc=1, device_id=peer, device_id_type=MESH)

    landing = iter(landings)
    partner = {
        (level, s, c): next(landing)
        for level in (ONE, TWO) for s in range(SECTIONS) for c in range(chunks)
    }
    for c in range(chunks):
        partner[ONE, LENT, c] = last.at[ONE, c]
        partner[TWO, SECTIONS, c] = last.at[TWO, c]

    loads = {}

    def load(name, src, dst):
        loads[name] = pltpu.make_async_copy(src, dst, in_sems.at[len(all_loads)])
        all_loads.append(name)
        loads[name].start()

    all_loads = []
    for c in range(chunks):
        columns = pl.ds(c * WIDTH, WIDTH)
        load(("x", c), field.at[:, :, columns], x.at[:, :, columns])
        if c == 0:
            load(("s", TWO), source_two, sources.at[TWO])
            load(("s", ONE), source_one, sources.at[ONE])

    def load_rest():
        load("tables", tables, table)
        for s in range(SECTIONS):
            if s < SECTIONS - 1:
                load(("w", ONE, s), sections_one.at[s], weights.at[ONE, s])
            load(("w", TWO, s), sections_two.at[s], weights.at[TWO, s])
        load(("t", ONE), target_one, targets.at[ONE])
        load(("t", TWO), target_two, targets.at[TWO])

    def need(name):
        if name in loads:
            loads.pop(name).wait()

    def move(level, stage, c):
        return pltpu.make_async_remote_copy(
            src_ref=own.at[level, 2 if (level, stage) == (ONE, LENT) else stage, c],
            dst_ref=partner[level, stage, c],
            send_sem=send_sems.at[level, stage, c],
            recv_sem=recv_sems.at[level, stage, c],
            device_id=peers[level, stage],
            device_id_type=MESH,
        )

    def lend(at, src, dst):
        return pltpu.make_async_remote_copy(
            src_ref=src,
            dst_ref=dst,
            send_sem=lent_send_sems.at[at],
            recv_sem=lent_recv_sems.at[at],
            device_id=peers[ONE, LENT],
            device_id_type=MESH,
        )

    lending = [lend(0, sections_one.at[SECTIONS - 1], lent), lend(1, tables, lent_table)]

    def start_leaves(level, c):
        need(("x", c))
        need(("s", level))

        @pl.loop(0, nodes)
        def _(n):
            block = x[n, :, c * WIDTH : (c + 1) * WIDTH]
            own[level, 0, c, n] = jnp.dot(
                sources[level, n], block, preferred_element_type=jnp.float32
            ).astype(jnp.bfloat16)

    def section(level, s, c):
        need(("w", level, s))
        need("tables")

        @pl.loop(0, nodes)
        def _(n):
            near = jnp.dot(
                weights[level, s, n, :, :leaf], own[level, s, c, n], preferred_element_type=jnp.float32
            )
            far = jnp.dot(
                weights[level, s, n, :, leaf:],
                partner[level, s, c][table[level, s, 0, 0, n]],
                preferred_element_type=jnp.float32,
            )
            own[level, s + 1, c, n] = (near + far).astype(jnp.bfloat16)

    def prepare(c):
        need(("t", TWO))

        @pl.loop(0, nodes)
        def _(n):
            near[n] = jnp.dot(lent[n, :, :leaf], last[ONE, c, n], preferred_element_type=jnp.float32)
            two[n] = jnp.dot(targets[TWO, n], last[TWO, c, n], preferred_element_type=jnp.float32)

    def finish(c):
        need(("t", ONE))
        for n in range(nodes):
            far = jnp.dot(
                lent[n, :, leaf:],
                partner[ONE, 2, c][lent_table[ONE, 2, 0, 0, n]],
                preferred_element_type=jnp.float32,
            )
            one[n] = (near[n] + far).astype(jnp.bfloat16)
        for n in range(nodes):
            product = jnp.dot(targets[ONE, n], one[n], preferred_element_type=jnp.float32)
            outs[n][:, c * WIDTH : (c + 1) * WIDTH] = (product + two[n]).astype(jnp.bfloat16)

    order = [(level, stage, c) for level, stage in CRITICAL for c in range(chunks)]
    moves = [
        (level, stage) for level in (ONE, TWO) for stage in range(STAGES) if (level, stage) != (ONE, 2)
    ]
    ready, sent, received = set(), 0, 0
    greeting = [True]

    def greet():
        if greeting:
            greeting.pop()
            pl.semaphore_wait(barrier, len(greeted))

    def push():
        nonlocal sent
        while sent < len(order) and order[sent] in ready and sent < received + WINDOW:
            greet()
            move(*order[sent]).start()
            sent += 1

    for c in range(chunks):
        start_leaves(TWO, c)
        ready.add((TWO, 0, c))
        push()
        start_leaves(ONE, c)
        move(ONE, 0, c).start()
        if c == 0:
            load_rest()
    for level, stage, c in arrivals(chunks):
        if (level, stage) == (ONE, 2):
            move(TWO, SECTIONS, c).wait_recv()
            if c == 0:
                for copy in lending:
                    copy.wait_recv()
            prepare(c)
            if c == chunks - 1:
                for copy in lending:
                    copy.wait_send()
                for at in range(chunks):
                    for there in moves:
                        move(*there, at).wait_send()
        move(level, stage, c).wait_recv()
        if (level, stage, c) in order:
            received += 1
            push()
        if (level, stage) == (ONE, LENT):
            continue
        if (level, stage) == (ONE, 2):
            finish(c)
            continue
        section(level, stage, c)
        if (level, stage, c) == (ONE, 0, chunks - 1):
            for copy in lending:
                copy.start()
        ready.add((level, stage + 1, c))
        push()
        if (level, stage) == (ONE, 1):
            move(ONE, LENT, c).start()
        if (level, stage + 1) not in CRITICAL:
            move(level, stage + 1, c).start()

    for c in range(chunks):
        move(ONE, 2, c).wait_send()


def on_device(
    field, source_one, sections_one, target_one, source_two, sections_two, target_two, pairing
):
    nodes, leaf = source_one.shape[2:4]
    columns = field.shape[3]
    chunks = columns // WIDTH
    top_bit = lax.axis_size("grp").bit_length() - 1
    anywhere = pl.BlockSpec(memory_space=pl.ANY)
    half = jnp.bfloat16
    blocks = (2, STAGES, chunks, nodes, leaf, WIDTH)
    results = pl.pallas_call(
        functools.partial(kernel, top_bit),
        out_shape=[jax.ShapeDtypeStruct((leaf, columns), half)] * nodes,
        in_specs=[anywhere] * 8,
        out_specs=[pl.BlockSpec(memory_space=pltpu.VMEM)] * nodes,
        scratch_shapes=[
            pltpu.VMEM((nodes, leaf, columns), half),
            pltpu.VMEM((2, nodes, leaf, leaf), half),
            pltpu.VMEM((2, SECTIONS, nodes, leaf, 2 * leaf), half),
            pltpu.VMEM((nodes, leaf, 2 * leaf), half),
            pltpu.VMEM((2, nodes, leaf, leaf), half),
            pltpu.VMEM(blocks, half),
            pltpu.VMEM((2, chunks, nodes, leaf, WIDTH), half),
            pltpu.VMEM((nodes, leaf, WIDTH), jnp.float32),
            pltpu.VMEM((nodes, leaf, WIDTH), half),
            pltpu.VMEM((nodes, leaf, WIDTH), jnp.float32),
            pltpu.SMEM(pairing.shape, pairing.dtype),
            pltpu.SMEM(pairing.shape, pairing.dtype),
            pltpu.SemaphoreType.DMA((chunks + 2 + 1 + 2 * SECTIONS - 1 + 2,)),
            pltpu.SemaphoreType.DMA((2, STAGES, chunks)),
            pltpu.SemaphoreType.DMA((2, STAGES, chunks)),
            pltpu.SemaphoreType.DMA((2,)),
            pltpu.SemaphoreType.DMA((2,)),
        ]
        + [pltpu.VMEM((nodes, leaf, WIDTH), half)] * (2 * SECTIONS * chunks),
        compiler_params=pltpu.CompilerParams(
            collective_id=0, has_side_effects=True, vmem_limit_bytes=105 << 19
        ),
        name="butterfly",
    )(
        field.reshape(nodes, leaf, columns),
        source_one[0, 0], sections_one[0, 0], target_one[0, 0],
        source_two[0, 0], sections_two[0, 0], target_two[0, 0],
        pairing,
    )
    return jnp.concatenate(results, axis=0).reshape(field.shape)


def solution(mesh):
    placed = (
        P("grp", "half", None, None),
        P("grp", "half", None, None, None),
        P("grp", "half", None, None, None, None),
        P("grp", "half", None, None, None),
        P("grp", "half", None, None, None),
        P("grp", "half", None, None, None, None),
        P("grp", "half", None, None, None),
        P(None, None, "grp", "half", None),
    )
    return jax.shard_map(
        on_device,
        mesh=mesh,
        in_specs=placed,
        out_specs=P("grp", "half", None, None),
        check_vma=False,
    )
```

```python
import functools

import jax
import jax.numpy as jnp
from jax import lax
from jax.experimental import pallas as pl
from jax.experimental.pallas import tpu as pltpu
from jax.sharding import PartitionSpec as P

SECTIONS = 3
STAGES = SECTIONS + 1
WIDTH = 128
MESH = pl.DeviceIdType.MESH
WINDOW = 2
ONE, TWO = 0, 1
CRITICAL = ((TWO, 0), (ONE, 1), (TWO, 1), (ONE, 2))
LENT = 3


def flipped(index, bit):
    size = 1 << bit
    return index + size - 2 * size * ((index // size) % 2)


def arrivals(chunks):
    due = []
    span = 2.0
    for place, (level, stage) in enumerate(CRITICAL):
        for c in range(chunks):
            due.append((span * (chunks * place + c + 1), level, stage, c))
    for c in range(chunks):
        due.append((c + 1.0 + 0.1, ONE, 0, c))
        done = span * (2 * chunks + c + 1)
        due.append((done + 1.5 * span, TWO, 2, c))
        due.append((span * (chunks + c + 1) + 1.5 * span, ONE, LENT, c))
    return [entry[1:] for entry in sorted(due)]


def kernel(
    top_bit, field, source_one, sections_one, target_one, source_two, sections_two, target_two, tables,
    *results_and_scratch,
):
    nodes = source_one.shape[0]
    outs = results_and_scratch[:nodes]
    (
        x, sources, weights, lent, targets, own, last, near, one, two, table, lent_table,
        in_sems, send_sems, recv_sems, lent_send_sems, lent_recv_sems, *landings,
    ) = results_and_scratch[nodes:]
    chunks = own.shape[2]
    leaf = x.shape[1]
    g, h = lax.axis_index("grp"), lax.axis_index("half")

    peers = {}
    for s in range(SECTIONS):
        peers[ONE, s] = (flipped(g, top_bit - 1 - s), h)
        peers[TWO, s] = (flipped(g, top_bit - 2 - s), h)
    peers[ONE, LENT] = (g, 1 - h)
    peers[TWO, SECTIONS] = (flipped(g, top_bit - 1), h)

    barrier = pltpu.get_barrier_semaphore()
    greeted = [peers[ONE, s] for s in range(STAGES)] + [peers[TWO, 2]]
    for peer in greeted:
        pl.semaphore_signal(barrier, inc=1, device_id=peer, device_id_type=MESH)

    landing = iter(landings)
    partner = {
        (level, s, c): next(landing)
        for level in (ONE, TWO) for s in range(SECTIONS) for c in range(chunks)
    }
    for c in range(chunks):
        partner[ONE, LENT, c] = last.at[ONE, c]
        partner[TWO, SECTIONS, c] = last.at[TWO, c]

    loads = {}

    def load(name, src, dst):
        loads[name] = pltpu.make_async_copy(src, dst, in_sems.at[len(all_loads)])
        all_loads.append(name)
        loads[name].start()

    all_loads = []
    for c in range(chunks):
        columns = pl.ds(c * WIDTH, WIDTH)
        load(("x", c), field.at[:, :, columns], x.at[:, :, columns])
        if c == 0:
            load(("s", TWO), source_two, sources.at[TWO])
            load(("s", ONE), source_one, sources.at[ONE])

    def load_rest():
        load("tables", tables, table)
        for s in range(SECTIONS):
            if s < SECTIONS - 1:
                load(("w", ONE, s), sections_one.at[s], weights.at[ONE, s])
            load(("w", TWO, s), sections_two.at[s], weights.at[TWO, s])
        load(("t", ONE), target_one, targets.at[ONE])
        load(("t", TWO), target_two, targets.at[TWO])

    def need(name):
        if name in loads:
            loads.pop(name).wait()

    def move(level, stage, c):
        source = own.at[level, stage, c]
        if (level, stage) == (ONE, LENT):
            source = own.at[ONE, 2, c]
        if (level, stage) == (ONE, 2):
            source = last.at[ONE, c]
        return pltpu.make_async_remote_copy(
            src_ref=source,
            dst_ref=partner[level, stage, c],
            send_sem=send_sems.at[level, stage, c],
            recv_sem=recv_sems.at[level, stage, c],
            device_id=peers[level, stage],
            device_id_type=MESH,
        )

    def lend(at, src, dst):
        return pltpu.make_async_remote_copy(
            src_ref=src,
            dst_ref=dst,
            send_sem=lent_send_sems.at[at],
            recv_sem=lent_recv_sems.at[at],
            device_id=peers[ONE, LENT],
            device_id_type=MESH,
        )

    lending = [lend(0, sections_one.at[SECTIONS - 1], lent), lend(1, tables, lent_table)]

    def start_leaves(level, c):
        need(("x", c))
        need(("s", level))

        @pl.loop(0, nodes)
        def _(n):
            block = x[n, :, c * WIDTH : (c + 1) * WIDTH]
            own[level, 0, c, n] = jnp.dot(
                sources[level, n], block, preferred_element_type=jnp.float32
            ).astype(jnp.bfloat16)

    def section(level, s, c):
        need(("w", level, s))
        need("tables")

        @pl.loop(0, nodes)
        def _(n):
            near = jnp.dot(
                weights[level, s, n, :, :leaf], own[level, s, c, n], preferred_element_type=jnp.float32
            )
            far = jnp.dot(
                weights[level, s, n, :, leaf:],
                partner[level, s, c][table[level, s, 0, 0, n]],
                preferred_element_type=jnp.float32,
            )
            own[level, s + 1, c, n] = (near + far).astype(jnp.bfloat16)

    def prepare(c):
        need(("t", TWO))

        @pl.loop(0, nodes)
        def _(n):
            near[n] = jnp.dot(lent[n, :, :leaf], last[ONE, c, n], preferred_element_type=jnp.float32)
            two[n] = jnp.dot(targets[TWO, n], last[TWO, c, n], preferred_element_type=jnp.float32)

    def finish(c):
        need(("t", ONE))
        for n in range(nodes):
            far = jnp.dot(
                lent[n, :, leaf:],
                partner[ONE, 2, c][lent_table[ONE, 2, 0, 0, n]],
                preferred_element_type=jnp.float32,
            )
            one[n] = (near[n] + far).astype(jnp.bfloat16)
        for n in range(nodes):
            product = jnp.dot(targets[ONE, n], one[n], preferred_element_type=jnp.float32)
            outs[n][:, c * WIDTH : (c + 1) * WIDTH] = (product + two[n]).astype(jnp.bfloat16)

    order = [(level, stage, c) for level, stage in CRITICAL for c in range(chunks)]
    moves = [
        (level, stage) for level in (ONE, TWO) for stage in range(STAGES) if (level, stage) != (ONE, 2)
    ]
    ready, sent, received = set(), 0, 0
    greeting = [True]

    def greet():
        if greeting:
            greeting.pop()
            pl.semaphore_wait(barrier, len(greeted))

    def push():
        nonlocal sent
        while sent < len(order) and order[sent] in ready and sent < received + WINDOW:
            greet()
            move(*order[sent]).start()
            sent += 1

    for c in range(chunks):
        start_leaves(TWO, c)
        ready.add((TWO, 0, c))
        push()
        start_leaves(ONE, c)
        move(ONE, 0, c).start()
        if c == 0:
            load_rest()
    for level, stage, c in arrivals(chunks):
        if (level, stage) == (ONE, 2):
            move(TWO, SECTIONS, c).wait_recv()
            if c == 0:
                for copy in lending:
                    copy.wait_recv()
            prepare(c)
            if c == chunks - 1:
                for copy in lending:
                    copy.wait_send()
                for at in range(chunks):
                    for there in moves:
                        move(*there, at).wait_send()
        move(level, stage, c).wait_recv()
        if (level, stage, c) in order:
            received += 1
            push()
        if (level, stage) == (ONE, LENT):
            ready.add((ONE, 2, c))
            push()
            continue
        if (level, stage) == (ONE, 2):
            finish(c)
            continue
        section(level, stage, c)
        if (level, stage, c) == (ONE, 0, chunks - 1):
            for copy in lending:
                copy.start()
        if (level, stage) == (ONE, 1):
            move(ONE, LENT, c).start()
            continue
        ready.add((level, stage + 1, c))
        push()
        if (level, stage + 1) not in CRITICAL:
            move(level, stage + 1, c).start()

    for c in range(chunks):
        move(ONE, 2, c).wait_send()


def on_device(
    field, source_one, sections_one, target_one, source_two, sections_two, target_two, pairing
):
    nodes, leaf = source_one.shape[2:4]
    columns = field.shape[3]
    chunks = columns // WIDTH
    top_bit = lax.axis_size("grp").bit_length() - 1
    anywhere = pl.BlockSpec(memory_space=pl.ANY)
    half = jnp.bfloat16
    blocks = (2, STAGES, chunks, nodes, leaf, WIDTH)
    results = pl.pallas_call(
        functools.partial(kernel, top_bit),
        out_shape=[jax.ShapeDtypeStruct((leaf, columns), half)] * nodes,
        in_specs=[anywhere] * 8,
        out_specs=[pl.BlockSpec(memory_space=pltpu.VMEM)] * nodes,
        scratch_shapes=[
            pltpu.VMEM((nodes, leaf, columns), half),
            pltpu.VMEM((2, nodes, leaf, leaf), half),
            pltpu.VMEM((2, SECTIONS, nodes, leaf, 2 * leaf), half),
            pltpu.VMEM((nodes, leaf, 2 * leaf), half),
            pltpu.VMEM((2, nodes, leaf, leaf), half),
            pltpu.VMEM(blocks, half),
            pltpu.VMEM((2, chunks, nodes, leaf, WIDTH), half),
            pltpu.VMEM((nodes, leaf, WIDTH), jnp.float32),
            pltpu.VMEM((nodes, leaf, WIDTH), half),
            pltpu.VMEM((nodes, leaf, WIDTH), jnp.float32),
            pltpu.SMEM(pairing.shape, pairing.dtype),
            pltpu.SMEM(pairing.shape, pairing.dtype),
            pltpu.SemaphoreType.DMA((chunks + 2 + 1 + 2 * SECTIONS - 1 + 2,)),
            pltpu.SemaphoreType.DMA((2, STAGES, chunks)),
            pltpu.SemaphoreType.DMA((2, STAGES, chunks)),
            pltpu.SemaphoreType.DMA((2,)),
            pltpu.SemaphoreType.DMA((2,)),
        ]
        + [pltpu.VMEM((nodes, leaf, WIDTH), half)] * (2 * SECTIONS * chunks),
        compiler_params=pltpu.CompilerParams(
            collective_id=0, has_side_effects=True, vmem_limit_bytes=105 << 19
        ),
        name="butterfly",
    )(
        field.reshape(nodes, leaf, columns),
        source_one[0, 0], sections_one[0, 0], target_one[0, 0],
        source_two[0, 0], sections_two[0, 0], target_two[0, 0],
        pairing,
    )
    return jnp.concatenate(results, axis=0).reshape(field.shape)


def solution(mesh):
    placed = (
        P("grp", "half", None, None),
        P("grp", "half", None, None, None),
        P("grp", "half", None, None, None, None),
        P("grp", "half", None, None, None),
        P("grp", "half", None, None, None),
        P("grp", "half", None, None, None, None),
        P("grp", "half", None, None, None),
        P(None, None, "grp", "half", None),
    )
    return jax.shard_map(
        on_device,
        mesh=mesh,
        in_specs=placed,
        out_specs=P("grp", "half", None, None),
        check_vma=False,
    )
```

```python
import functools

import jax
import jax.numpy as jnp
from jax import lax
from jax.experimental import pallas as pl
from jax.experimental.pallas import tpu as pltpu
from jax.sharding import PartitionSpec as P

SECTIONS = 3
STAGES = SECTIONS + 1
WIDTH = 128
MESH = pl.DeviceIdType.MESH
WINDOW = 2
ONE, TWO = 0, 1
CRITICAL = ((TWO, 0), (ONE, 1), (TWO, 1), (ONE, 2))
LENT = 3


def flipped(index, bit):
    size = 1 << bit
    return index + size - 2 * size * ((index // size) % 2)


def arrivals(chunks):
    due = []
    span = 2.0
    for place, (level, stage) in enumerate(CRITICAL):
        for c in range(chunks):
            due.append((span * (chunks * place + c + 1), level, stage, c))
    for c in range(chunks):
        due.append((c + 1.0 + 0.1, ONE, 0, c))
        done = span * (2 * chunks + c + 1)
        due.append((done + 1.5 * span, TWO, 2, c))
        due.append((span * (chunks + c + 1) + 1.5 * span, ONE, LENT, c))
    return [entry[1:] for entry in sorted(due)]


def kernel(
    top_bit, field, source_one, sections_one, target_one, source_two, sections_two, target_two, tables,
    *results_and_scratch,
):
    nodes = source_one.shape[0]
    outs = results_and_scratch[:nodes]
    (
        x, sources, weights, lent, targets, own, last, near, one, two, table, lent_table,
        in_sems, send_sems, recv_sems, lent_send_sems, lent_recv_sems, *landings,
    ) = results_and_scratch[nodes:]
    chunks = own.shape[2]
    leaf = x.shape[1]
    g, h = lax.axis_index("grp"), lax.axis_index("half")

    peers = {}
    for s in range(SECTIONS):
        peers[ONE, s] = (flipped(g, top_bit - 1 - s), h)
        peers[TWO, s] = (flipped(g, top_bit - 2 - s), h)
    peers[ONE, LENT] = (g, 1 - h)
    peers[TWO, SECTIONS] = (flipped(g, top_bit - 1), h)

    barrier = pltpu.get_barrier_semaphore()
    greeted = [peers[ONE, s] for s in range(STAGES)] + [peers[TWO, 2]]
    for peer in greeted:
        pl.semaphore_signal(barrier, inc=1, device_id=peer, device_id_type=MESH)

    landing = iter(landings)
    partner = {
        (level, s, c): next(landing)
        for level in (ONE, TWO) for s in range(SECTIONS) for c in range(chunks)
    }
    for c in range(chunks):
        partner[ONE, LENT, c] = last.at[ONE, c]
        partner[TWO, SECTIONS, c] = last.at[TWO, c]

    loads = {}

    def load(name, src, dst):
        loads[name] = pltpu.make_async_copy(src, dst, in_sems.at[len(all_loads)])
        all_loads.append(name)
        loads[name].start()

    all_loads = []
    for c in range(chunks):
        columns = pl.ds(c * WIDTH, WIDTH)
        load(("x", c), field.at[:, :, columns], x.at[:, :, columns])
        if c == 0:
            load(("s", TWO), source_two, sources.at[TWO])
            load(("s", ONE), source_one, sources.at[ONE])

    def load_rest():
        load("tables", tables, table)
        for s in range(SECTIONS):
            if s < SECTIONS - 1:
                load(("w", ONE, s), sections_one.at[s], weights.at[ONE, s])
            load(("w", TWO, s), sections_two.at[s], weights.at[TWO, s])
        load(("t", ONE), target_one, targets.at[ONE])
        load(("t", TWO), target_two, targets.at[TWO])

    def need(name):
        if name in loads:
            loads.pop(name).wait()

    def move(level, stage, c):
        source = own.at[level, stage, c]
        if (level, stage) == (ONE, LENT):
            source = own.at[ONE, 2, c]
        if (level, stage) == (ONE, 2):
            source = last.at[ONE, c]
        return pltpu.make_async_remote_copy(
            src_ref=source,
            dst_ref=partner[level, stage, c],
            send_sem=send_sems.at[level, stage, c],
            recv_sem=recv_sems.at[level, stage, c],
            device_id=peers[level, stage],
            device_id_type=MESH,
        )

    def lend(at, src, dst):
        return pltpu.make_async_remote_copy(
            src_ref=src,
            dst_ref=dst,
            send_sem=lent_send_sems.at[at],
            recv_sem=lent_recv_sems.at[at],
            device_id=peers[ONE, LENT],
            device_id_type=MESH,
        )

    lending = [lend(0, sections_one.at[SECTIONS - 1], lent), lend(1, tables, lent_table)]

    def start_leaves(level, c):
        need(("x", c))
        need(("s", level))

        @pl.loop(0, nodes, unroll=c == 0)
        def _(n):
            block = x[n, :, c * WIDTH : (c + 1) * WIDTH]
            own[level, 0, c, n] = jnp.dot(
                sources[level, n], block, preferred_element_type=jnp.float32
            ).astype(jnp.bfloat16)

    def section(level, s, c):
        need(("w", level, s))
        need("tables")

        @pl.loop(0, nodes)
        def _(n):
            near = jnp.dot(
                weights[level, s, n, :, :leaf], own[level, s, c, n], preferred_element_type=jnp.float32
            )
            far = jnp.dot(
                weights[level, s, n, :, leaf:],
                partner[level, s, c][table[level, s, 0, 0, n]],
                preferred_element_type=jnp.float32,
            )
            own[level, s + 1, c, n] = (near + far).astype(jnp.bfloat16)

    def prepare(c):
        need(("t", TWO))

        @pl.loop(0, nodes)
        def _(n):
            near[n] = jnp.dot(lent[n, :, :leaf], last[ONE, c, n], preferred_element_type=jnp.float32)
            two[n] = jnp.dot(targets[TWO, n], last[TWO, c, n], preferred_element_type=jnp.float32)

    def finish(c):
        need(("t", ONE))
        for n in range(nodes):
            far = jnp.dot(
                lent[n, :, leaf:],
                partner[ONE, 2, c][lent_table[ONE, 2, 0, 0, n]],
                preferred_element_type=jnp.float32,
            )
            one[n] = (near[n] + far).astype(jnp.bfloat16)
        for n in range(nodes):
            product = jnp.dot(targets[ONE, n], one[n], preferred_element_type=jnp.float32)
            outs[n][:, c * WIDTH : (c + 1) * WIDTH] = (product + two[n]).astype(jnp.bfloat16)

    order = [(level, stage, c) for level, stage in CRITICAL for c in range(chunks)]
    moves = [
        (level, stage) for level in (ONE, TWO) for stage in range(STAGES) if (level, stage) != (ONE, 2)
    ]
    ready, sent, received = set(), 0, 0
    greeting = [True]

    def greet():
        if greeting:
            greeting.pop()
            pl.semaphore_wait(barrier, len(greeted))

    def push():
        nonlocal sent
        while sent < len(order) and order[sent] in ready and sent < received + WINDOW:
            greet()
            move(*order[sent]).start()
            sent += 1

    for c in range(chunks):
        start_leaves(TWO, c)
        ready.add((TWO, 0, c))
        push()
        start_leaves(ONE, c)
        move(ONE, 0, c).start()
        if c == 0:
            load_rest()
    for level, stage, c in arrivals(chunks):
        if (level, stage) == (ONE, 2):
            move(TWO, SECTIONS, c).wait_recv()
            if c == 0:
                for copy in lending:
                    copy.wait_recv()
            prepare(c)
            if c == chunks - 1:
                for copy in lending:
                    copy.wait_send()
                for at in range(chunks):
                    for there in moves:
                        move(*there, at).wait_send()
        move(level, stage, c).wait_recv()
        if (level, stage, c) in order:
            received += 1
            push()
        if (level, stage) == (ONE, LENT):
            ready.add((ONE, 2, c))
            push()
            continue
        if (level, stage) == (ONE, 2):
            finish(c)
            continue
        section(level, stage, c)
        if (level, stage, c) == (ONE, 0, chunks - 1):
            for copy in lending:
                copy.start()
        if (level, stage) == (ONE, 1):
            move(ONE, LENT, c).start()
            continue
        ready.add((level, stage + 1, c))
        push()
        if (level, stage + 1) not in CRITICAL:
            move(level, stage + 1, c).start()

    for c in range(chunks):
        move(ONE, 2, c).wait_send()


def on_device(
    field, source_one, sections_one, target_one, source_two, sections_two, target_two, pairing
):
    nodes, leaf = source_one.shape[2:4]
    columns = field.shape[3]
    chunks = columns // WIDTH
    top_bit = lax.axis_size("grp").bit_length() - 1
    anywhere = pl.BlockSpec(memory_space=pl.ANY)
    half = jnp.bfloat16
    blocks = (2, STAGES, chunks, nodes, leaf, WIDTH)
    results = pl.pallas_call(
        functools.partial(kernel, top_bit),
        out_shape=[jax.ShapeDtypeStruct((leaf, columns), half)] * nodes,
        in_specs=[anywhere] * 8,
        out_specs=[pl.BlockSpec(memory_space=pltpu.VMEM)] * nodes,
        scratch_shapes=[
            pltpu.VMEM((nodes, leaf, columns), half),
            pltpu.VMEM((2, nodes, leaf, leaf), half),
            pltpu.VMEM((2, SECTIONS, nodes, leaf, 2 * leaf), half),
            pltpu.VMEM((nodes, leaf, 2 * leaf), half),
            pltpu.VMEM((2, nodes, leaf, leaf), half),
            pltpu.VMEM(blocks, half),
            pltpu.VMEM((2, chunks, nodes, leaf, WIDTH), half),
            pltpu.VMEM((nodes, leaf, WIDTH), jnp.float32),
            pltpu.VMEM((nodes, leaf, WIDTH), half),
            pltpu.VMEM((nodes, leaf, WIDTH), jnp.float32),
            pltpu.SMEM(pairing.shape, pairing.dtype),
            pltpu.SMEM(pairing.shape, pairing.dtype),
            pltpu.SemaphoreType.DMA((chunks + 2 + 1 + 2 * SECTIONS - 1 + 2,)),
            pltpu.SemaphoreType.DMA((2, STAGES, chunks)),
            pltpu.SemaphoreType.DMA((2, STAGES, chunks)),
            pltpu.SemaphoreType.DMA((2,)),
            pltpu.SemaphoreType.DMA((2,)),
        ]
        + [pltpu.VMEM((nodes, leaf, WIDTH), half)] * (2 * SECTIONS * chunks),
        compiler_params=pltpu.CompilerParams(
            collective_id=0, has_side_effects=True, vmem_limit_bytes=105 << 19
        ),
        name="butterfly",
    )(
        field.reshape(nodes, leaf, columns),
        source_one[0, 0], sections_one[0, 0], target_one[0, 0],
        source_two[0, 0], sections_two[0, 0], target_two[0, 0],
        pairing,
    )
    return jnp.concatenate(results, axis=0).reshape(field.shape)


def solution(mesh):
    placed = (
        P("grp", "half", None, None),
        P("grp", "half", None, None, None),
        P("grp", "half", None, None, None, None),
        P("grp", "half", None, None, None),
        P("grp", "half", None, None, None),
        P("grp", "half", None, None, None, None),
        P("grp", "half", None, None, None),
        P(None, None, "grp", "half", None),
    )
    return jax.shard_map(
        on_device,
        mesh=mesh,
        in_specs=placed,
        out_specs=P("grp", "half", None, None),
        check_vma=False,
    )
```

```python
import functools

import jax
import jax.numpy as jnp
from jax import lax
from jax.experimental import pallas as pl
from jax.experimental.pallas import tpu as pltpu
from jax.sharding import PartitionSpec as P

SECTIONS = 3
STAGES = SECTIONS + 1
WIDTH = 128
MESH = pl.DeviceIdType.MESH
WINDOW = 2
ONE, TWO = 0, 1
CRITICAL = ((TWO, 0), (ONE, 1), (TWO, 1), (ONE, 2))
LENT = 3


def flipped(index, bit):
    size = 1 << bit
    return index + size - 2 * size * ((index // size) % 2)


def arrivals(chunks):
    due = []
    span = 2.0
    for place, (level, stage) in enumerate(CRITICAL):
        for c in range(chunks):
            due.append((span * (chunks * place + c + 1), level, stage, c))
    for c in range(chunks):
        due.append((c + 1.0 + 0.1, ONE, 0, c))
        done = span * (2 * chunks + c + 1)
        due.append((done + 1.5 * span, TWO, 2, c))
        due.append((span * (chunks + c + 1) + 1.5 * span, ONE, LENT, c))
    return [entry[1:] for entry in sorted(due)]


def kernel(
    top_bit, field, source_one, sections_one, target_one, source_two, sections_two, target_two, tables,
    *results_and_scratch,
):
    nodes = source_one.shape[0]
    outs = results_and_scratch[:nodes]
    (
        x, sources, weights, lent, targets, own, last, near, one, two, table, lent_table,
        in_sems, send_sems, recv_sems, lent_send_sems, lent_recv_sems, *landings,
    ) = results_and_scratch[nodes:]
    chunks = own.shape[2]
    leaf = x.shape[1]
    g, h = lax.axis_index("grp"), lax.axis_index("half")

    peers = {}
    for s in range(SECTIONS):
        peers[ONE, s] = (flipped(g, top_bit - 1 - s), h)
        peers[TWO, s] = (flipped(g, top_bit - 2 - s), h)
    peers[ONE, LENT] = (g, 1 - h)
    peers[TWO, SECTIONS] = (flipped(g, top_bit - 1), h)

    barrier = pltpu.get_barrier_semaphore()
    greeted = [peers[ONE, s] for s in range(STAGES)] + [peers[TWO, 2]]
    for peer in greeted:
        pl.semaphore_signal(barrier, inc=1, device_id=peer, device_id_type=MESH)

    landing = iter(landings)
    partner = {
        (level, s, c): next(landing)
        for level in (ONE, TWO) for s in range(SECTIONS) for c in range(chunks)
    }
    for c in range(chunks):
        partner[ONE, LENT, c] = last.at[ONE, c]
        partner[TWO, SECTIONS, c] = last.at[TWO, c]

    loads = {}

    def load(name, src, dst):
        loads[name] = pltpu.make_async_copy(src, dst, in_sems.at[len(all_loads)])
        all_loads.append(name)
        loads[name].start()

    all_loads = []
    def load_field(c):
        columns = pl.ds(c * WIDTH, WIDTH)
        load(("x", c), field.at[:, :, columns], x.at[:, :, columns])

    load_field(0)
    load(("s", TWO), source_two, sources.at[TWO])

    def load_rest():
        load(("s", ONE), source_one, sources.at[ONE])
        for c in range(1, chunks):
            load_field(c)
        load("tables", tables, table)
        for s in range(SECTIONS):
            if s < SECTIONS - 1:
                load(("w", ONE, s), sections_one.at[s], weights.at[ONE, s])
            load(("w", TWO, s), sections_two.at[s], weights.at[TWO, s])
        load(("t", ONE), target_one, targets.at[ONE])
        load(("t", TWO), target_two, targets.at[TWO])

    def need(name):
        if name in loads:
            loads.pop(name).wait()

    def move(level, stage, c):
        source = own.at[level, stage, c]
        if (level, stage) == (ONE, LENT):
            source = own.at[ONE, 2, c]
        if (level, stage) == (ONE, 2):
            source = last.at[ONE, c]
        return pltpu.make_async_remote_copy(
            src_ref=source,
            dst_ref=partner[level, stage, c],
            send_sem=send_sems.at[level, stage, c],
            recv_sem=recv_sems.at[level, stage, c],
            device_id=peers[level, stage],
            device_id_type=MESH,
        )

    def lend(at, src, dst):
        return pltpu.make_async_remote_copy(
            src_ref=src,
            dst_ref=dst,
            send_sem=lent_send_sems.at[at],
            recv_sem=lent_recv_sems.at[at],
            device_id=peers[ONE, LENT],
            device_id_type=MESH,
        )

    lending = [lend(0, sections_one.at[SECTIONS - 1], lent), lend(1, tables, lent_table)]

    def start_leaves(level, c):
        need(("x", c))
        need(("s", level))

        @pl.loop(0, nodes)
        def _(n):
            block = x[n, :, c * WIDTH : (c + 1) * WIDTH]
            own[level, 0, c, n] = jnp.dot(
                sources[level, n], block, preferred_element_type=jnp.float32
            ).astype(jnp.bfloat16)

    def section(level, s, c):
        need(("w", level, s))
        need("tables")

        @pl.loop(0, nodes)
        def _(n):
            near = jnp.dot(
                weights[level, s, n, :, :leaf], own[level, s, c, n], preferred_element_type=jnp.float32
            )
            far = jnp.dot(
                weights[level, s, n, :, leaf:],
                partner[level, s, c][table[level, s, 0, 0, n]],
                preferred_element_type=jnp.float32,
            )
            own[level, s + 1, c, n] = (near + far).astype(jnp.bfloat16)

    def prepare(c):
        need(("t", TWO))

        @pl.loop(0, nodes)
        def _(n):
            near[n] = jnp.dot(lent[n, :, :leaf], last[ONE, c, n], preferred_element_type=jnp.float32)
            two[n] = jnp.dot(targets[TWO, n], last[TWO, c, n], preferred_element_type=jnp.float32)

    def finish(c):
        need(("t", ONE))
        for n in range(nodes):
            far = jnp.dot(
                lent[n, :, leaf:],
                partner[ONE, 2, c][lent_table[ONE, 2, 0, 0, n]],
                preferred_element_type=jnp.float32,
            )
            one[n] = (near[n] + far).astype(jnp.bfloat16)
        for n in range(nodes):
            product = jnp.dot(targets[ONE, n], one[n], preferred_element_type=jnp.float32)
            outs[n][:, c * WIDTH : (c + 1) * WIDTH] = (product + two[n]).astype(jnp.bfloat16)

    order = [(level, stage, c) for level, stage in CRITICAL for c in range(chunks)]
    moves = [
        (level, stage) for level in (ONE, TWO) for stage in range(STAGES) if (level, stage) != (ONE, 2)
    ]
    ready, sent, received = set(), 0, 0
    greeting = [True]

    def greet():
        if greeting:
            greeting.pop()
            pl.semaphore_wait(barrier, len(greeted))

    def push():
        nonlocal sent
        while sent < len(order) and order[sent] in ready and sent < received + WINDOW:
            greet()
            move(*order[sent]).start()
            sent += 1

    for c in range(chunks):
        start_leaves(TWO, c)
        ready.add((TWO, 0, c))
        push()
        if c == 0:
            load_rest()
        start_leaves(ONE, c)
        move(ONE, 0, c).start()
    for level, stage, c in arrivals(chunks):
        if (level, stage) == (ONE, 2):
            move(TWO, SECTIONS, c).wait_recv()
            if c == 0:
                for copy in lending:
                    copy.wait_recv()
            prepare(c)
            if c == chunks - 1:
                for copy in lending:
                    copy.wait_send()
                for at in range(chunks):
                    for there in moves:
                        move(*there, at).wait_send()
        move(level, stage, c).wait_recv()
        if (level, stage, c) in order:
            received += 1
            push()
        if (level, stage) == (ONE, LENT):
            ready.add((ONE, 2, c))
            push()
            continue
        if (level, stage) == (ONE, 2):
            finish(c)
            continue
        section(level, stage, c)
        if (level, stage, c) == (ONE, 0, chunks - 1):
            for copy in lending:
                copy.start()
        if (level, stage) == (ONE, 1):
            move(ONE, LENT, c).start()
            continue
        ready.add((level, stage + 1, c))
        push()
        if (level, stage + 1) not in CRITICAL:
            move(level, stage + 1, c).start()

    for c in range(chunks):
        move(ONE, 2, c).wait_send()


def on_device(
    field, source_one, sections_one, target_one, source_two, sections_two, target_two, pairing
):
    nodes, leaf = source_one.shape[2:4]
    columns = field.shape[3]
    chunks = columns // WIDTH
    top_bit = lax.axis_size("grp").bit_length() - 1
    anywhere = pl.BlockSpec(memory_space=pl.ANY)
    half = jnp.bfloat16
    blocks = (2, STAGES, chunks, nodes, leaf, WIDTH)
    results = pl.pallas_call(
        functools.partial(kernel, top_bit),
        out_shape=[jax.ShapeDtypeStruct((leaf, columns), half)] * nodes,
        in_specs=[anywhere] * 8,
        out_specs=[pl.BlockSpec(memory_space=pltpu.VMEM)] * nodes,
        scratch_shapes=[
            pltpu.VMEM((nodes, leaf, columns), half),
            pltpu.VMEM((2, nodes, leaf, leaf), half),
            pltpu.VMEM((2, SECTIONS, nodes, leaf, 2 * leaf), half),
            pltpu.VMEM((nodes, leaf, 2 * leaf), half),
            pltpu.VMEM((2, nodes, leaf, leaf), half),
            pltpu.VMEM(blocks, half),
            pltpu.VMEM((2, chunks, nodes, leaf, WIDTH), half),
            pltpu.VMEM((nodes, leaf, WIDTH), jnp.float32),
            pltpu.VMEM((nodes, leaf, WIDTH), half),
            pltpu.VMEM((nodes, leaf, WIDTH), jnp.float32),
            pltpu.SMEM(pairing.shape, pairing.dtype),
            pltpu.SMEM(pairing.shape, pairing.dtype),
            pltpu.SemaphoreType.DMA((chunks + 2 + 1 + 2 * SECTIONS - 1 + 2,)),
            pltpu.SemaphoreType.DMA((2, STAGES, chunks)),
            pltpu.SemaphoreType.DMA((2, STAGES, chunks)),
            pltpu.SemaphoreType.DMA((2,)),
            pltpu.SemaphoreType.DMA((2,)),
        ]
        + [pltpu.VMEM((nodes, leaf, WIDTH), half)] * (2 * SECTIONS * chunks),
        compiler_params=pltpu.CompilerParams(
            collective_id=0, has_side_effects=True, vmem_limit_bytes=105 << 19
        ),
        name="butterfly",
    )(
        field.reshape(nodes, leaf, columns),
        source_one[0, 0], sections_one[0, 0], target_one[0, 0],
        source_two[0, 0], sections_two[0, 0], target_two[0, 0],
        pairing,
    )
    return jnp.concatenate(results, axis=0).reshape(field.shape)


def solution(mesh):
    placed = (
        P("grp", "half", None, None),
        P("grp", "half", None, None, None),
        P("grp", "half", None, None, None, None),
        P("grp", "half", None, None, None),
        P("grp", "half", None, None, None),
        P("grp", "half", None, None, None, None),
        P("grp", "half", None, None, None),
        P(None, None, "grp", "half", None),
    )
    return jax.shard_map(
        on_device,
        mesh=mesh,
        in_specs=placed,
        out_specs=P("grp", "half", None, None),
        check_vma=False,
    )
```
